512 devices in a mesh: seq: 32 (over z_hi, x, core), chan: 16 (over z_lo, y).
Axes of the slice: x: 4, y: 4, z: 16 (z_hi: 4, z_lo: 4; z = z_hi * 4 + z_lo), core: 2. Of those that a mesh axis runs over, the one named last changes fastest.
Arguments:
- tokens: bfloat16 [3, 1024, 131072], P(None, 'chan', 'seq'), may hold values from -6 to 6
- kernel: bfloat16 [1024, 131072], P('chan', 'seq'), may hold values from -6 to 6
- left_factor: bfloat16 [512, 512], replicated, may hold values from -0.25 to 0.25
- right_factor: bfloat16 [256, 256], replicated, may hold values from -0.375 to 0.375
- norm_gain: float32 [1024], replicated, may hold values from 0.1 to 1.9
- up_weight: bfloat16 [4, 256, 1024], P(None, None, 'seq'), may hold values from -0.375 to 0.375
- down_weight: bfloat16 [4, 1024, 256], P(None, 'seq'), may hold values from -0.1875 to 0.1875
Outputs:
- layer_out: bfloat16 [3, 131072, 1024], P(None, ('seq', 'chan'))
The draws below stay inside these ranges and needn't reach their ends.
All inputs are finite; a program needn't handle non-finite values.
Results may differ from the reference program's by a relative error of at most 0.0057.
Values may be sent and summed in bfloat16 or wider, within the bound.
No kernel may reach another device: no remote copies, remote signals or barrier semaphores. Data moves between devices by JAX's collectives and lax.ppermute only.
A program may use at most 64 MiB of HBM per device.

```python
import jax
import jax.numpy as jnp
from jax import lax

D = 1024
BLK = 512
BROWS = 256
BATCH = 3
GROUPS = 4
SEQLEN = 131072


def steps_of(stream_key, dims, shards, smallest, largest):
    factor_of, own = 1.0, jax.random.fold_in(stream_key, 6)
    for axis_at, shards_of in shards:
        steps = jnp.exp(jax.random.uniform(jax.random.fold_in(own, axis_at), (shards_of,), jnp.float32, smallest / len(shards), largest / len(shards)))
        factor_of = factor_of * jnp.repeat(steps, dims[axis_at] // shards_of).reshape([-1 if axis == axis_at else 1 for axis in range(len(dims))])
    return factor_of


def noise(stream_key, shape, deviation, reach, cuts=(), kind=jnp.bfloat16):
    gain = steps_of(stream_key, shape, cuts, -0.22, 0.18) if cuts else 1.0
    array = jax.random.normal(stream_key, shape, jnp.float32) * deviation * gain
    return jnp.minimum(jnp.maximum(array, -reach), reach).astype(kind)


def setup_inputs(seed: int = 0) -> dict:
    seeds = jax.random.split(jax.random.key(seed), 8)
    tokens = noise(seeds[0], (BATCH, D, SEQLEN), 1.0, 6.0, ((1, 16), (2, 32)))
    kernel = noise(seeds[1], (D, SEQLEN), 1.0, 6.0, ((0, 16), (1, 32)))
    left_factor = noise(seeds[2], (BLK, BLK), BLK ** -0.5, 0.25)
    right_factor = noise(seeds[3], (BROWS, BROWS), BROWS ** -0.5, 0.375)
    norm_gain = jnp.clip(1.0 + 0.18 * jax.random.normal(seeds[4], (D,), jnp.float32), 0.1, 1.9)
    up_weight = noise(seeds[5], (GROUPS, D // GROUPS, D), (D // GROUPS) ** -0.5, 0.375, ((2, 32),))
    down_weight = noise(seeds[6], (GROUPS, D, D // GROUPS), D ** -0.5, 0.1875, ((1, 32),))
    return {"tokens": tokens, "kernel": kernel, "left_factor": left_factor, "right_factor": right_factor, "norm_gain": norm_gain, "up_weight": up_weight, "down_weight": down_weight}


def mix_block(pair, left_factor, right_factor):
    xb, kb = pair
    chans = xb.shape[0]
    xflat = xb.astype(jnp.float32)
    x3 = xflat.reshape(chans, BROWS, BLK)
    first = jnp.einsum('cab,bj->caj', x3, left_factor.astype(jnp.float32))
    middle = (first * kb.reshape(chans, BROWS, BLK).astype(jnp.float32)).astype(jnp.bfloat16)
    second = jnp.einsum('caj,ak->cjk', middle.astype(jnp.float32), right_factor.astype(jnp.float32))
    gated = (xflat + jax.nn.sigmoid(xflat) * second.reshape(chans, BROWS * BLK)).astype(jnp.bfloat16)
    return gated

def mlp_block(rows, norm_gain, up_weight, down_weight):
    count = rows.shape[0]
    hf = rows.astype(jnp.float32)
    mean = lax.optimization_barrier(jnp.mean(hf, axis=1, keepdims=True))
    var = lax.optimization_barrier(jnp.mean((hf - mean) ** 2, axis=1, keepdims=True))
    normed = ((hf - mean) * lax.rsqrt(var + 1e-05) * norm_gain).astype(jnp.bfloat16)
    z4 = normed.reshape(count, GROUPS, D // GROUPS).astype(jnp.float32)
    hidden = jax.nn.gelu(jnp.einsum('tgr,grm->tgm', z4, up_weight.astype(jnp.float32))).astype(jnp.bfloat16)
    regrouped = hidden.reshape(count, GROUPS, GROUPS, D // GROUPS).transpose(0, 2, 1, 3).reshape(count, GROUPS, D)
    down = jnp.einsum('thn,hnr->thr', regrouped.astype(jnp.float32), down_weight.astype(jnp.float32))
    return (hf + down.reshape(count, D)).astype(jnp.bfloat16)

def reference(tokens, kernel, left_factor, right_factor, norm_gain, up_weight, down_weight):
    cblock = 32
    tblock = 4096
    ks = kernel.reshape(D // cblock, cblock, BROWS * BLK)
    results = []
    for seq_index in range(BATCH):
        xs = tokens[seq_index].reshape(D // cblock, cblock, BROWS * BLK)
        gated = lax.map(lambda pair: mix_block(pair, left_factor, right_factor), (xs, ks))
        rows = gated.reshape(D, BROWS * BLK).T
        out = lax.map(lambda r: mlp_block(r, norm_gain, up_weight, down_weight), rows.reshape(BROWS * BLK // tblock, tblock, D))
        results.append(out.reshape(BROWS * BLK, D))
    return jnp.stack(results)
```

```python
import jax
import jax.numpy as jnp
from jax import lax
from jax.experimental import pallas as pl
from jax.experimental.pallas import tpu as pltpu
from jax.sharding import PartitionSpec as P

F32 = jnp.float32
BF16 = jnp.bfloat16
SEQ = 32
CHAN = 16
ROWS = 8
BLK = 512
BROWS = 256
CH = 64
GROUPS = 4
PARAMS = pltpu.CompilerParams(vmem_limit_bytes=48 * 1024 * 1024)


def first_kernel(tok_ref, ker_ref, left_ref, out_ref, pair_ref, last_ref):
    left_t = left_ref[...].astype(F32).T.astype(BF16)

    def piece(ref, lead, a):
        if lead is None:
            return ref[:, a * BLK:(a + 1) * BLK]
        return ref[lead, :, a * BLK:(a + 1) * BLK]

    def matmul_t(x):
        return lax.dot_general(left_t, x, (((1,), (1,)), ((), ())), preferred_element_type=F32)

    for quad in range(ROWS // 4):
        rows = range(quad * 4, quad * 4 + 4)
        taps = jnp.concatenate([piece(ker_ref, None, a) for a in rows], axis=0).astype(F32).T
        prod = matmul_t(jnp.concatenate([piece(tok_ref, 2, a) for a in rows], axis=0)) * taps
        for i, a in enumerate(rows):
            one = prod[:, i * CH:(i + 1) * CH].reshape(SEQ, 2, 8, CH)
            for jh in range(2):
                last_ref[a * 256:(a + 1) * 256, jh * CH:(jh + 1) * CH] = one[:, jh].reshape(256, CH)
        for i in range(2):
            two = [quad * 4 + 2 * i, quad * 4 + 2 * i + 1]
            stacked = [piece(tok_ref, n, a) for a in two for n in range(2)]
            prod = matmul_t(jnp.concatenate(stacked, axis=0))
            for k, a in enumerate(two):
                tap = taps[:, (2 * i + k) * CH:(2 * i + k + 1) * CH]
                tap2 = jnp.concatenate([tap, tap], axis=1)
                pair_ref[a * BLK:(a + 1) * BLK, :] = prod[:, k * 128:(k + 1) * 128] * tap2
    for dst in range(SEQ):
        for jl in range(8):
            both = [pair_ref[pl.ds(dst * 16 + jh * 8 + jl, 8, stride=BLK), :] for jh in range(2)]
            out_ref[dst, :, jl * 128:(jl + 1) * 128] = jnp.concatenate(both, axis=0).astype(BF16)
        for jq in range(4):
            both = [last_ref[pl.ds(dst * 8 + jm * 4 + jq, 8, stride=256), :] for jm in range(2)]
            out_ref[dst, :, 1024 + jq * 128:1024 + (jq + 1) * 128] = jnp.concatenate(both, axis=0).astype(BF16)


def gate(x, mixed):
    x = x.astype(F32)
    return (x + (0.5 * jnp.tanh(0.5 * x) + 0.5) * mixed).astype(BF16)


def second_kernel(mid_ref, right_ref, tok_ref, out_ref):
    right = right_ref[...].astype(F32).reshape(SEQ, ROWS, BROWS)
    zero = jnp.zeros_like(right)
    upper = jnp.concatenate([right, zero], axis=1).reshape(512, BROWS)
    lower = jnp.concatenate([zero, right], axis=1).reshape(512, BROWS)
    wide = jnp.concatenate([upper, lower], axis=1).astype(BF16)

    def mix(at):
        rows = mid_ref[:, :, at * 128:(at + 1) * 128].reshape(512, 128)
        return lax.dot_general(rows, wide, (((0,), (0,)), ((), ())), preferred_element_type=F32)

    def put(n, j, value):
        x = tok_ref[n, :, j * BROWS:(j + 1) * BROWS]
        out_ref[j, :, n * BROWS:(n + 1) * BROWS] = gate(x, value)

    for jl in range(8):
        mixed = mix(jl)
        for n in range(2):
            for jh in range(2):
                put(n, jh * 8 + jl, mixed[n * CH:(n + 1) * CH, jh * BROWS:(jh + 1) * BROWS])
    for jq in range(4):
        mixed = mix(8 + jq)
        for jh in range(2):
            for jm in range(2):
                put(2, jh * 8 + jm * 4 + jq, mixed[jh * CH:(jh + 1) * CH, jm * BROWS:(jm + 1) * BROWS])


def mlp_kernel(x_ref, gain_ref, w_ref, out_ref):
    width = CHAN * CH
    x = x_ref[...].reshape(width, BROWS).astype(F32).T
    mean = jnp.mean(x, axis=1, keepdims=True)
    cent = x - mean
    var = jnp.mean(cent * cent, axis=1, keepdims=True)
    normed = (cent * lax.rsqrt(var + 1e-05) * gain_ref[...]).astype(BF16)
    acc = [None] * GROUPS
    for g in range(GROUPS):
        part = normed[:, g * 256:(g + 1) * 256]
        for h in range(GROUPS):
            up = w_ref[h * 8:(h + 1) * 8, 0, g].reshape(256, 256)
            value = lax.dot_general(part, up, (((1,), (1,)), ((), ())), preferred_element_type=F32)
            hidden = jax.nn.gelu(value).astype(BF16)
            down = w_ref[g * 8:(g + 1) * 8, 1, h].reshape(256, 256)
            term = jnp.dot(hidden, down, preferred_element_type=F32)
            acc[h] = term if acc[h] is None else acc[h] + term
    for h in range(GROUPS):
        out_ref[0, :, h * 256:(h + 1) * 256] = (x[:, h * 256:(h + 1) * 256] + acc[h]).astype(BF16)


def per_device(tokens, kernel, left_factor, right_factor, norm_gain, up_weight, down_weight):
    weights = jnp.stack([up_weight.transpose(0, 2, 1), down_weight])
    weights = lax.all_gather(weights, "seq", axis=0)
    middle = pl.pallas_call(
        first_kernel,
        out_shape=jax.ShapeDtypeStruct((SEQ, 16, 1536), BF16),
        scratch_shapes=[pltpu.VMEM((ROWS * BLK, 128), F32), pltpu.VMEM((ROWS * 256, 128), F32)],
        compiler_params=PARAMS,
        name="first",
    )(tokens, kernel, left_factor)
    middle = lax.all_to_all(middle, "seq", 0, 0, tiled=True)
    gated = pl.pallas_call(
        second_kernel,
        out_shape=jax.ShapeDtypeStruct((CHAN, CH, 3 * BROWS), BF16),
        compiler_params=PARAMS,
        name="second",
    )(middle, right_factor, tokens)
    gated = lax.all_to_all(gated, "chan", 0, 0, tiled=True)
    return pl.pallas_call(
        mlp_kernel,
        grid=(3,),
        in_specs=[
            pl.BlockSpec((CHAN, CH, BROWS), lambda n: (0, 0, n)),
            pl.BlockSpec((1, CHAN * CH), lambda n: (0, 0)),
            pl.BlockSpec((SEQ, 2, GROUPS, 32, 256), lambda n: (0, 0, 0, 0, 0)),
        ],
        out_specs=pl.BlockSpec((1, BROWS, CHAN * CH), lambda n: (n, 0, 0)),
        out_shape=jax.ShapeDtypeStruct((3, BROWS, CHAN * CH), BF16),
        compiler_params=PARAMS,
        name="mlp",
    )(gated, norm_gain.reshape(1, CHAN * CH), weights)


def solution(mesh):
    placed = (
        P(None, "chan", "seq"),
        P("chan", "seq"),
        P(),
        P(),
        P(),
        P(None, None, "seq"),
        P(None, "seq", None),
    )
    return jax.shard_map(
        per_device,
        mesh=mesh,
        in_specs=placed,
        out_specs=P(None, ("seq", "chan"), None),
        check_vma=False,
    )
```

```python
import jax
import jax.numpy as jnp
from jax import lax
from jax.experimental import pallas as pl
from jax.experimental.pallas import tpu as pltpu
from jax.sharding import PartitionSpec as P

F32 = jnp.float32
BF16 = jnp.bfloat16
SEQ = 32
CHAN = 16
ROWS = 8
BLK = 512
BROWS = 256
CH = 64
GROUPS = 4
SEQ_AXES = ("z_hi", "x", "core")
CHAN_AXES = ("z_lo", "y")
PARAMS = pltpu.CompilerParams(vmem_limit_bytes=60 * 1024 * 1024)
WEIGHTS = 128
ANY = pl.BlockSpec(memory_space=pl.ANY)


def rows_of(ref, lead, a):
    return ref[:, a * BLK:(a + 1) * BLK] if lead is None else ref[lead, :, a * BLK:(a + 1) * BLK]


def matmul_t(left_t, x):
    return lax.dot_general(left_t, x, (((1,), (1,)), ((), ())), preferred_element_type=F32)


def transposed(ref):
    return ref[...].astype(F32).T.astype(BF16)


def first_last_kernel(tok_ref, ker_ref, left_ref, up_ref, down_ref, *refs):
    *outs, work_ref = refs
    own_z, own_x, own_core = lax.axis_index("z_hi"), lax.axis_index("x"), lax.axis_index("core")
    left_t = transposed(left_ref)
    for quad in range(ROWS // 4):
        rows = range(quad * 4, quad * 4 + 4)
        taps = jnp.concatenate([rows_of(ker_ref, None, a) for a in rows], axis=0).astype(F32).T
        prod = matmul_t(left_t, jnp.concatenate([rows_of(tok_ref, 0, a) for a in rows], axis=0)) * taps
        for i, a in enumerate(rows):
            one = prod[:, i * CH:(i + 1) * CH].reshape(SEQ, 2, 8, CH)
            for jh in range(2):
                work_ref[a * 256:(a + 1) * 256, jh * CH:(jh + 1) * CH] = one[:, jh].reshape(256, CH)
    own_y = lax.axis_index("y")
    for step in range(4):
        for kind, ref in enumerate((up_ref, down_ref)):
            for i in range(2):
                outs[step][8 + kind, :, i * 256:(i + 1) * 256] = ref[own_y, i * 16:(i + 1) * 16, :]
        for x_step in range(4):
            for core_step in range(2):
                core = own_core if core_step == 0 else 1 - own_core
                dst = lax.rem(own_z + step, 4) * 8 + lax.rem(own_x + x_step, 4) * 2 + core
                for jq in range(4):
                    both = [work_ref[pl.ds(dst * 8 + (jm * 4 + jq), 8, stride=256), :] for jm in range(2)]
                    block = jnp.concatenate(both, axis=0).astype(BF16)
                    outs[step][x_step * 2 + core_step, :, jq * 128:(jq + 1) * 128] = block


def first_pair_kernel(tok_ref, ker_ref, left_ref, out_ref, work_ref):
    left_t = transposed(left_ref)
    for quad in range(ROWS // 4):
        rows = range(quad * 4, quad * 4 + 4)
        taps = jnp.concatenate([rows_of(ker_ref, None, a) for a in rows], axis=0).astype(F32).T
        for i in range(2):
            two = [quad * 4 + 2 * i, quad * 4 + 2 * i + 1]
            prod = matmul_t(left_t, jnp.concatenate([rows_of(tok_ref, n, a) for a in two for n in range(2)], axis=0))
            for k, a in enumerate(two):
                tap = taps[:, (2 * i + k) * CH:(2 * i + k + 1) * CH]
                tap2 = jnp.concatenate([tap, tap], axis=1)
                work_ref[a * BLK:(a + 1) * BLK, :] = prod[:, k * 128:(k + 1) * 128] * tap2
    for dst in range(SEQ):
        for jl in range(8):
            both = [work_ref[pl.ds(dst * 16 + jh * 8 + jl, 8, stride=BLK), :] for jh in range(2)]
            out_ref[dst, :, jl * 128:(jl + 1) * 128] = jnp.concatenate(both, axis=0).astype(BF16)


def z_join_kernel(*refs):
    parts, outs = refs[:4], refs[4:]
    for x_step, out in enumerate(outs):
        for step, part in enumerate(parts):
            for core_step in range(2):
                out[core_step * 4 + step] = part[x_step * 2 + core_step]
            out[8 + 2 * step:10 + 2 * step] = part[8:10]


def x_join_kernel(*refs):
    *parts, weights, blocks = refs
    for i, part in enumerate(parts):
        weights[8 * i:8 * i + 8] = part[8:16]
        blocks[4 * i:4 * i + 4] = part[4:8]


def y_join_kernel(*refs):
    *parts, out = refs
    for i, part in enumerate(parts):
        out[32 * i:32 * i + 32] = part[...]


def gate(x, mixed):
    x = x.astype(F32)
    return (x + (0.5 * jnp.tanh(0.5 * x) + 0.5) * mixed).astype(BF16)


def mix(rows, wide):
    return lax.dot_general(rows, wide, (((0,), (0,)), ((), ())), preferred_element_type=F32)


def second_last_kernel(*refs):
    parts, far_ref, right_ref, tok_ref, out_ref, wide_ref = refs[:4], *refs[4:]
    own_z, own_x, own_core = lax.axis_index("z_hi"), lax.axis_index("x"), lax.axis_index("core")
    wide_ref[...] = jnp.zeros_like(wide_ref)
    for i in range(32):
        core = own_core if i < 16 else 1 - own_core
        x, z = lax.rem(own_x + 4 - i // 4 % 4, 4), lax.rem(own_z + 4 - i % 4, 4)
        at = pl.multiple_of((z * 8 + x * 2 + core) * 8, 8)
        rows = right_ref[pl.ds(at, 8), :]
        wide_ref[i * 16:i * 16 + 8, :BROWS] = rows
        wide_ref[i * 16 + 8:i * 16 + 16, BROWS:] = rows
    wide = wide_ref[...].astype(BF16)
    for jq in range(4):
        lanes = slice(jq * 128, (jq + 1) * 128)
        rows = [part[:4, :, lanes].reshape(64, 128) for part in parts] + [far_ref[:, :, lanes].reshape(256, 128)]
        mixed = mix(jnp.concatenate(rows, axis=0), wide)
        for jh in range(2):
            for jm in range(2):
                j = jh * 8 + jm * 4 + jq
                x = tok_ref[0, :, j * BROWS:(j + 1) * BROWS]
                out_ref[j] = gate(x, mixed[jh * CH:(jh + 1) * CH, jm * BROWS:(jm + 1) * BROWS])


def second_pair_kernel(mid_ref, right_ref, tok_ref, kept_ref, out_ref):
    right = right_ref[...].reshape(SEQ, ROWS, BROWS)
    zero = jnp.zeros_like(right)
    upper = jnp.concatenate([right, zero], axis=1).reshape(512, BROWS)
    lower = jnp.concatenate([zero, right], axis=1).reshape(512, BROWS)
    wide = jnp.concatenate([upper, lower], axis=1).astype(BF16)
    for jl in range(8):
        mixed = mix(mid_ref[:, :, jl * 128:(jl + 1) * 128].reshape(512, 128), wide)
        for n in range(2):
            for jh in range(2):
                j = jh * 8 + jl
                x = tok_ref[n, :, j * BROWS:(j + 1) * BROWS]
                value = mixed[n * CH:(n + 1) * CH, jh * BROWS:(jh + 1) * BROWS]
                out_ref[j, :, n * BROWS:(n + 1) * BROWS] = gate(x, value)


def mlp_kernel(x_ref, gain_ref, near_ref, far_ref, out_ref):
    x = x_ref[...].reshape(CHAN * CH, BROWS).astype(F32).T
    mean = jnp.mean(x, axis=1, keepdims=True)
    cent = x - mean
    var = jnp.mean(cent * cent, axis=1, keepdims=True)
    normed = (cent * lax.rsqrt(var + 1e-05) * gain_ref[...]).astype(BF16)
    own_y, own_z = lax.axis_index("y"), lax.axis_index("z_hi")

    def weight(y, z, kind):
        base = lax.rem(own_y + 4 - y, 4) * 32 + lax.rem(own_z + 4 - z, 4) * 2 + kind
        blocks = [ref[base + x_step * 8] for ref in (near_ref, far_ref) for x_step in range(4)]
        return jnp.concatenate([block[:, i * 256:(i + 1) * 256] for block in blocks for i in range(2)], axis=0)

    acc = [None] * GROUPS
    for g in range(GROUPS):
        part = normed[:, g * 256:(g + 1) * 256]
        for h in range(GROUPS):
            value = matmul_t(part, weight(g, h, 0))
            hidden = jax.nn.gelu(value).astype(BF16)
            term = jnp.dot(hidden, weight(h, g, 1), preferred_element_type=F32)
            acc[h] = term if acc[h] is None else acc[h] + term
    for h in range(GROUPS):
        out_ref[0, :, h * 256:(h + 1) * 256] = (x[:, h * 256:(h + 1) * 256] + acc[h]).astype(BF16)


def shift(x, axis, step, size=4):
    return lax.ppermute(x, axis, [(i, (i + step) % size) for i in range(size)])


def spread(parts, axis):
    return [parts[0]] + [shift(parts[step], axis, step) for step in (1, 2, 3)]


def shape(*dims):
    return jax.ShapeDtypeStruct(dims, BF16)


def whole(*dims):
    return pl.BlockSpec(dims, lambda i: (0,) * len(dims))


def join(kernel, out_shape, name, *args, flops=0):
    return pl.pallas_call(
        kernel,
        out_shape=out_shape,
        compiler_params=PARAMS,
        cost_estimate=pl.CostEstimate(flops=flops, bytes_accessed=0, transcendentals=0),
        name=name,
    )(*args)


def per_device(tokens, kernel, left_factor, right_factor, norm_gain, up_weight, down_weight):
    chans = tokens.shape[1]
    local = tokens.shape[2]
    parts = pl.pallas_call(
        first_last_kernel,
        grid=(1,),
        in_specs=[
            pl.BlockSpec((1, chans, local), lambda i: (2, 0, 0)),
            whole(chans, local),
            whole(BLK, BLK),
            whole(GROUPS, 32, 256),
            whole(GROUPS, 32, 256),
        ],
        out_specs=[whole(10, 16, 512)] * 4,
        out_shape=[shape(10, 16, 512)] * 4,
        scratch_shapes=[pltpu.VMEM((ROWS * 256, 128), F32)],
        compiler_params=PARAMS,
        name="first_last",
    )(tokens, kernel, left_factor, up_weight.transpose(0, 2, 1), down_weight)
    parts = spread(parts, "z_hi")
    middle = pl.pallas_call(
        first_pair_kernel,
        grid=(1,),
        in_specs=[
            pl.BlockSpec((2, chans, local), lambda i: (0, 0, 0)),
            whole(chans, local),
            whole(BLK, BLK),
        ],
        out_specs=whole(SEQ, 16, 1024),
        out_shape=shape(SEQ, 16, 1024),
        scratch_shapes=[pltpu.VMEM((ROWS * BLK, 128), F32)],
        compiler_params=PARAMS,
        name="first_pair",
    )(tokens, kernel, left_factor)
    middle = lax.all_to_all(middle, SEQ_AXES, 0, 0, tiled=True)

    parts = join(z_join_kernel, [shape(16, 16, 512)] * 4, "z_join", *parts, flops=200 * 10**9)
    parts = spread(parts, "x")
    weights, blocks = join(x_join_kernel, [shape(32, 16, 512), shape(16, 16, 512)], "x_join", *parts)
    blocks = lax.ppermute(blocks, "core", [(0, 1), (1, 0)])
    near = join(y_join_kernel, shape(WEIGHTS, 16, 512), "y_join", *spread([weights] * 4, "y"), flops=200 * 10**9)
    far = lax.ppermute(near, "core", [(0, 1), (1, 0)])

    right = right_factor.astype(F32)
    gated = pl.pallas_call(
        second_last_kernel,
        grid=(1,),
        in_specs=[
            whole(16, 16, 512),
            whole(16, 16, 512),
            whole(16, 16, 512),
            whole(16, 16, 512),
            whole(16, 16, 512),
            whole(BROWS, BROWS),
            pl.BlockSpec((1, chans, local), lambda i: (2, 0, 0)),
        ],
        out_specs=pl.BlockSpec((CHAN, CH, BROWS), lambda i: (0, 0, 2)),
        out_shape=shape(CHAN, CH, 3 * BROWS),
        scratch_shapes=[pltpu.VMEM((512, 512), F32)],
        compiler_params=PARAMS,
        name="second_last",
    )(*parts, blocks, right, tokens)
    gated = pl.pallas_call(
        second_pair_kernel,
        grid=(1,),
        in_specs=[
            whole(SEQ, 16, 1024),
            whole(BROWS, BROWS),
            pl.BlockSpec((2, chans, local), lambda i: (0, 0, 0)),
            ANY,
        ],
        out_specs=pl.BlockSpec((CHAN, CH, 2 * BROWS), lambda i: (0, 0, 0)),
        out_shape=shape(CHAN, CH, 3 * BROWS),
        input_output_aliases={3: 0},
        compiler_params=PARAMS,
        name="second_pair",
    )(middle, right, tokens, gated)
    gated = lax.all_to_all(gated, CHAN_AXES, 0, 0, tiled=True)
    return pl.pallas_call(
        mlp_kernel,
        grid=(3,),
        in_specs=[
            pl.BlockSpec((CHAN, CH, BROWS), lambda n: (0, 0, n)),
            pl.BlockSpec((1, CHAN * CH), lambda n: (0, 0)),
            pl.BlockSpec((WEIGHTS, 16, 512), lambda n: (0, 0, 0)),
            pl.BlockSpec((WEIGHTS, 16, 512), lambda n: (0, 0, 0)),
        ],
        out_specs=pl.BlockSpec((1, BROWS, CHAN * CH), lambda n: (n, 0, 0)),
        out_shape=shape(3, BROWS, CHAN * CH),
        compiler_params=PARAMS,
        name="mlp",
    )(gated, norm_gain.reshape(1, CHAN * CH), near, far)


def solution(mesh):
    fine = jax.sharding.Mesh(mesh.devices.reshape(4, 4, 2, 4, 4), SEQ_AXES + CHAN_AXES)
    placed = (
        P(None, CHAN_AXES, SEQ_AXES),
        P(CHAN_AXES, SEQ_AXES),
        P(),
        P(),
        P(),
        P(None, None, SEQ_AXES),
        P(None, SEQ_AXES, None),
    )
    return jax.shard_map(
        per_device,
        mesh=fine,
        in_specs=placed,
        out_specs=P(None, SEQ_AXES + CHAN_AXES, None),
        check_vma=False,
    )
```

```python
import jax
import jax.numpy as jnp
from jax import lax
from jax.experimental import pallas as pl
from jax.experimental.pallas import tpu as pltpu
from jax.sharding import PartitionSpec as P

F32 = jnp.float32
BF16 = jnp.bfloat16
SEQ = 32
CHAN = 16
ROWS = 8
BLK = 512
BROWS = 256
CH = 64
GROUPS = 4
SEQ_AXES = ("z_hi", "x", "core")
CHAN_AXES = ("z_lo", "y")
PARAMS = pltpu.CompilerParams(vmem_limit_bytes=60 * 1024 * 1024)
SMALL = pltpu.CompilerParams(vmem_limit_bytes=24 * 1024 * 1024)
WEIGHTS = 128
ANY = pl.BlockSpec(memory_space=pl.ANY)


def rows_of(ref, lead, a):
    return ref[:, a * BLK:(a + 1) * BLK] if lead is None else ref[lead, :, a * BLK:(a + 1) * BLK]


def matmul_t(left_t, x):
    return lax.dot_general(left_t, x, (((1,), (1,)), ((), ())), preferred_element_type=F32)


def transposed(ref):
    return ref[...].astype(F32).T.astype(BF16)


def first_last_kernel(tok_ref, ker_ref, left_ref, up_ref, down_ref, *refs):
    *outs, work_ref = refs
    own_z, own_x, own_core = lax.axis_index("z_hi"), lax.axis_index("x"), lax.axis_index("core")
    left_t = transposed(left_ref)
    for quad in range(ROWS // 4):
        rows = range(quad * 4, quad * 4 + 4)
        taps = jnp.concatenate([rows_of(ker_ref, None, a) for a in rows], axis=0).astype(F32).T
        prod = matmul_t(left_t, jnp.concatenate([rows_of(tok_ref, 0, a) for a in rows], axis=0)) * taps
        for i, a in enumerate(rows):
            one = prod[:, i * CH:(i + 1) * CH].reshape(SEQ, 2, 8, CH)
            for jh in range(2):
                work_ref[a * 256:(a + 1) * 256, jh * CH:(jh + 1) * CH] = one[:, jh].reshape(256, CH)
    own_y = lax.axis_index("y")
    for step in range(4):
        for kind, ref in enumerate((up_ref, down_ref)):
            for i in range(2):
                outs[step][8 + kind, :, i * 256:(i + 1) * 256] = ref[own_y, i * 16:(i + 1) * 16, :]
        for x_step in range(4):
            for core_step in range(2):
                core = own_core if core_step == 0 else 1 - own_core
                dst = lax.rem(own_z + step, 4) * 8 + lax.rem(own_x + x_step, 4) * 2 + core
                for jq in range(4):
                    both = [work_ref[pl.ds(dst * 8 + (jm * 4 + jq), 8, stride=256), :] for jm in range(2)]
                    block = jnp.concatenate(both, axis=0).astype(BF16)
                    outs[step][x_step * 2 + core_step, :, jq * 128:(jq + 1) * 128] = block


def first_pair_kernel(tok_ref, ker_ref, left_ref, out_ref, work_ref):
    left_t = transposed(left_ref)
    for quad in range(ROWS // 4):
        rows = range(quad * 4, quad * 4 + 4)
        taps = jnp.concatenate([rows_of(ker_ref, None, a) for a in rows], axis=0).astype(F32).T
        for i in range(2):
            two = [quad * 4 + 2 * i, quad * 4 + 2 * i + 1]
            prod = matmul_t(left_t, jnp.concatenate([rows_of(tok_ref, n, a) for a in two for n in range(2)], axis=0))
            for k, a in enumerate(two):
                tap = taps[:, (2 * i + k) * CH:(2 * i + k + 1) * CH]
                tap2 = jnp.concatenate([tap, tap], axis=1)
                work_ref[a * BLK:(a + 1) * BLK, :] = prod[:, k * 128:(k + 1) * 128] * tap2
    for dst in range(SEQ):
        for jl in range(8):
            both = [work_ref[pl.ds(dst * 16 + jh * 8 + jl, 8, stride=BLK), :] for jh in range(2)]
            out_ref[dst, :, jl * 128:(jl + 1) * 128] = jnp.concatenate(both, axis=0).astype(BF16)


def z_join_kernel(*refs):
    parts, outs, weights = refs[:4], refs[4:8], refs[8]
    for step, part in enumerate(parts):
        for x_step, out in enumerate(outs):
            for core_step in range(2):
                out[core_step * 4 + step] = part[x_step * 2 + core_step]
        weights[2 * step:2 * step + 2] = part[8:10]


def plane_join_kernel(*refs):
    parts, weights, out, joined = refs[:4], refs[4:8], refs[8], refs[9]
    for i, part in enumerate(parts):
        out[4 * i:4 * i + 4] = part[4:8]
    for i, part in enumerate(weights):
        joined[8 * i:8 * i + 8] = part[...]


def join_kernel(*refs):
    *parts, out = refs
    size = parts[0].shape[0]
    for i, part in enumerate(parts):
        out[size * i:size * (i + 1)] = part[...]


def gate(x, mixed):
    x = x.astype(F32)
    return (x + (0.5 * jnp.tanh(0.5 * x) + 0.5) * mixed).astype(BF16)


def mix(rows, wide):
    return lax.dot_general(rows, wide, (((0,), (0,)), ((), ())), preferred_element_type=F32)


def second_last_kernel(*refs):
    parts, far_ref, right_ref, tok_hbm, out_ref, wide_ref, copy_ref, tok_ref, sem = refs[:4], *refs[4:]
    own_z, own_x, own_core = lax.axis_index("z_hi"), lax.axis_index("x"), lax.axis_index("core")
    load = pltpu.make_async_copy(tok_hbm.at[2], tok_ref, sem)
    load.start()
    wide_ref[...] = jnp.zeros_like(wide_ref)
    copy_ref[...] = right_ref[...].astype(F32)
    for i in range(32):
        core = own_core if i < 16 else 1 - own_core
        x, z = lax.rem(own_x + 4 - i // 4 % 4, 4), lax.rem(own_z + 4 - i % 4, 4)
        at = pl.multiple_of((z * 8 + x * 2 + core) * 8, 8)
        rows = copy_ref[pl.ds(at, 8), :]
        wide_ref[i * 16:i * 16 + 8, :BROWS] = rows
        wide_ref[i * 16 + 8:i * 16 + 16, BROWS:] = rows
    wide = wide_ref[...].astype(BF16)
    load.wait()
    for jq in range(4):
        lanes = slice(jq * 128, (jq + 1) * 128)
        rows = [part[:4, :, lanes].reshape(64, 128) for part in parts] + [far_ref[:, :, lanes].reshape(256, 128)]
        mixed = mix(jnp.concatenate(rows, axis=0), wide)
        for jh in range(2):
            for jm in range(2):
                j = jh * 8 + jm * 4 + jq
                x = tok_ref[:, j * BROWS:(j + 1) * BROWS]
                out_ref[jh, jm * 4 + jq] = gate(x, mixed[jh * CH:(jh + 1) * CH, jm * BROWS:(jm + 1) * BROWS])


def second_pair_kernel(mid_ref, right_ref, tok_ref, kept_ref, out_ref):
    right = right_ref[...].astype(F32).reshape(SEQ, ROWS, BROWS)
    zero = jnp.zeros_like(right)
    upper = jnp.concatenate([right, zero], axis=1).reshape(512, BROWS)
    lower = jnp.concatenate([zero, right], axis=1).reshape(512, BROWS)
    wide = jnp.concatenate([upper, lower], axis=1).astype(BF16)
    for jl in range(8):
        mixed = mix(mid_ref[:, :, jl * 128:(jl + 1) * 128].reshape(512, 128), wide)
        for n in range(2):
            for jh in range(2):
                j = jh * 8 + jl
                x = tok_ref[n, :, j * BROWS:(j + 1) * BROWS]
                value = mixed[n * CH:(n + 1) * CH, jh * BROWS:(jh + 1) * BROWS]
                out_ref[jh, jl, :, n * BROWS:(n + 1) * BROWS] = gate(x, value)


def twice_gelu(x):
    return x + x * jnp.tanh(x * (0.7978845608028654 + 0.035677408136300125 * (x * x)))


def mlp_kernel(x_hbm, gain_ref, near_hbm, far_hbm, out_hbm, x_ref, rows_ref, normed_ref, out_ref, weight_ref, *sems):
    in_sems, weight_sems, out_sems = sems
    loads = [
        pltpu.make_async_copy(x_hbm.at[:, :, pl.ds(n * BROWS, BROWS)], x_ref.at[n], in_sems.at[n]) for n in range(3)
    ]
    weights = [
        pltpu.make_async_copy(share, weight_ref.at[pl.ds(core * WEIGHTS, WEIGHTS)], weight_sems.at[core])
        for core, share in enumerate((near_hbm, far_hbm))
    ]
    for load in loads + weights:
        load.start()
    for n, load in enumerate(loads):
        load.wait()
        rows = x_ref[n].reshape(CHAN * CH, BROWS).T
        x = rows.astype(F32)
        mean = jnp.mean(x, axis=1, keepdims=True)
        cent = x - mean
        var = jnp.mean(cent * cent, axis=1, keepdims=True)
        normed = (cent * lax.rsqrt(var + 1e-05) * gain_ref[...]).astype(BF16)
        rows_ref[n * BROWS:(n + 1) * BROWS, :] = rows
        normed_ref[n * BROWS:(n + 1) * BROWS, :] = normed
    own_y, own_z = lax.axis_index("y"), lax.axis_index("z_hi")

    def weight(y, z, kind):
        base = lax.rem(own_y + 4 - y, 4) * 8 + lax.rem(own_z + 4 - z, 4) * 2 + kind
        blocks = [weight_ref[base + step * 32] for step in range(8)]
        return jnp.concatenate([block[:, i * 256:(i + 1) * 256] for block in blocks for i in range(2)], axis=0)

    for load in weights:
        load.wait()
    stores = []
    for h in range(GROUPS):
        lanes = slice(h * 256, (h + 1) * 256)
        hidden = [
            twice_gelu(matmul_t(normed_ref[:, g * 256:(g + 1) * 256], weight(g, h, 0))).astype(BF16)
            for g in range(GROUPS)
        ]
        down = jnp.concatenate([weight(h, g, 1) for g in range(GROUPS)], axis=0)
        acc = jnp.dot(jnp.concatenate(hidden, axis=1), down, preferred_element_type=F32)
        out = (rows_ref[:, lanes].astype(F32) + 0.5 * acc).astype(BF16)
        out_ref[:, :, lanes] = out.reshape(3, BROWS, 256)
        at = pl.ds(h * 256, 256)
        stores.append(pltpu.make_async_copy(out_ref.at[:, :, at], out_hbm.at[:, :, at], out_sems.at[h]))
        stores[h].start()
    for store in stores:
        store.wait()


def shift(x, axis, step, size=4):
    return lax.ppermute(x, axis, [(i, (i + step) % size) for i in range(size)])


def spread(parts, axis):
    return [parts[0]] + [shift(parts[step], axis, step) for step in (1, 2, 3)]


def shape(*dims):
    return jax.ShapeDtypeStruct(dims, BF16)


def whole(*dims):
    return pl.BlockSpec(dims, lambda i: (0,) * len(dims))


def join(kernel, out_shape, name, *args, flops=0):
    return pl.pallas_call(
        kernel,
        out_shape=out_shape,
        compiler_params=pltpu.CompilerParams(vmem_limit_bytes=16 * 1024 * 1024),
        cost_estimate=pl.CostEstimate(flops=flops, bytes_accessed=0, transcendentals=0),
        name=name,
    )(*args)


def per_device(tokens, kernel, left_factor, right_factor, norm_gain, up_weight, down_weight):
    chans = tokens.shape[1]
    local = tokens.shape[2]
    parts = pl.pallas_call(
        first_last_kernel,
        grid=(1,),
        in_specs=[
            pl.BlockSpec((1, chans, local), lambda i: (2, 0, 0)),
            whole(chans, local),
            whole(BLK, BLK),
            whole(GROUPS, 32, 256),
            whole(GROUPS, 32, 256),
        ],
        out_specs=[whole(10, 16, 512)] * 4,
        out_shape=[shape(10, 16, 512)] * 4,
        scratch_shapes=[pltpu.VMEM((ROWS * 256, 128), F32)],
        compiler_params=PARAMS,
        name="first_last",
    )(tokens, kernel, left_factor, up_weight.transpose(0, 2, 1), down_weight)
    parts = spread(parts, "z_hi")
    middle = pl.pallas_call(
        first_pair_kernel,
        grid=(1,),
        in_specs=[
            pl.BlockSpec((2, chans, local), lambda i: (0, 0, 0)),
            whole(chans, local),
            whole(BLK, BLK),
        ],
        out_specs=whole(SEQ, 16, 1024),
        out_shape=shape(SEQ, 16, 1024),
        scratch_shapes=[pltpu.VMEM((ROWS * BLK, 128), F32)],
        compiler_params=PARAMS,
        name="first_pair",
    )(tokens, kernel, left_factor)
    middle = lax.all_to_all(middle, SEQ_AXES, 0, 0, tiled=True)

    *parts, weights = join(z_join_kernel, [shape(8, 16, 512)] * 5, "z_join", *parts, flops=200 * 10**9)
    parts = spread(parts, "x")
    weights = spread([weights] * 4, "y")
    blocks, weights = join(plane_join_kernel, [shape(16, 16, 512), shape(32, 16, 512)], "plane_join", *parts, *weights)
    blocks = lax.ppermute(blocks, "core", [(0, 1), (1, 0)])
    blocks, weights = lax.optimization_barrier((blocks, weights))
    near = join(join_kernel, shape(WEIGHTS, 16, 512), "x_join", *spread([weights] * 4, "x"), flops=200 * 10**9)
    far = lax.ppermute(near, "core", [(0, 1), (1, 0)])

    gated = pl.pallas_call(
        second_last_kernel,
        grid=(1,),
        in_specs=[
            whole(8, 16, 512),
            whole(8, 16, 512),
            whole(8, 16, 512),
            whole(8, 16, 512),
            whole(16, 16, 512),
            whole(BROWS, BROWS),
            ANY,
        ],
        out_specs=pl.BlockSpec((2, 8, CH, BROWS), lambda i: (0, 0, 0, 2)),
        out_shape=shape(2, 8, CH, 3 * BROWS),
        scratch_shapes=[
            pltpu.VMEM((512, 512), F32),
            pltpu.VMEM((BROWS, BROWS), F32),
            pltpu.VMEM((chans, local), BF16),
            pltpu.SemaphoreType.DMA,
        ],
        compiler_params=SMALL,
        name="second_last",
    )(*parts, blocks, right_factor, tokens)
    gated = pl.pallas_call(
        second_pair_kernel,
        grid=(1,),
        in_specs=[
            whole(SEQ, 16, 1024),
            whole(BROWS, BROWS),
            pl.BlockSpec((2, chans, local), lambda i: (0, 0, 0)),
            ANY,
        ],
        out_specs=pl.BlockSpec((2, 8, CH, 2 * BROWS), lambda i: (0, 0, 0, 0)),
        out_shape=shape(2, 8, CH, 3 * BROWS),
        input_output_aliases={3: 0},
        compiler_params=SMALL,
        name="second_pair",
    )(middle, right_factor, tokens, gated)
    gated = gated.reshape(CHAN, CH, 3 * BROWS)
    gated = lax.all_to_all(gated, CHAN_AXES, 0, 0, tiled=True)
    vmem = pl.BlockSpec(memory_space=pltpu.VMEM)
    width = CHAN * CH
    return pl.pallas_call(
        mlp_kernel,
        in_specs=[ANY, vmem, ANY, ANY],
        out_specs=ANY,
        out_shape=shape(3, BROWS, width),
        scratch_shapes=[
            pltpu.VMEM((3, CHAN, CH, BROWS), BF16),
            pltpu.VMEM((3 * BROWS, width), BF16),
            pltpu.VMEM((3 * BROWS, width), BF16),
            pltpu.VMEM((3, BROWS, width), BF16),
            pltpu.VMEM((2 * WEIGHTS, 16, 512), BF16),
            pltpu.SemaphoreType.DMA((3,)),
            pltpu.SemaphoreType.DMA((2,)),
            pltpu.SemaphoreType.DMA((GROUPS,)),
        ],
        compiler_params=PARAMS,
        name="mlp",
    )(gated, norm_gain.reshape(1, width), near, far)


def solution(mesh):
    fine = jax.sharding.Mesh(mesh.devices.reshape(4, 4, 2, 4, 4), SEQ_AXES + CHAN_AXES)
    placed = (
        P(None, CHAN_AXES, SEQ_AXES),
        P(CHAN_AXES, SEQ_AXES),
        P(),
        P(),
        P(),
        P(None, None, SEQ_AXES),
        P(None, SEQ_AXES, None),
    )
    return jax.shard_map(
        per_device,
        mesh=fine,
        in_specs=placed,
        out_specs=P(None, SEQ_AXES + CHAN_AXES, None),
        check_vma=False,
    )
```

```python
import jax
import jax.numpy as jnp
from jax import lax
from jax.experimental import pallas as pl
from jax.experimental.pallas import tpu as pltpu
from jax.sharding import PartitionSpec as P

F32 = jnp.float32
BF16 = jnp.bfloat16
SEQ = 32
CHAN = 16
ROWS = 8
BLK = 512
BROWS = 256
CH = 64
GROUPS = 4
SEQ_AXES = ("z_hi", "x", "core")
CHAN_AXES = ("z_lo", "y")
PARAMS = pltpu.CompilerParams(vmem_limit_bytes=60 * 1024 * 1024)
SMALL = pltpu.CompilerParams(vmem_limit_bytes=24 * 1024 * 1024)
WEIGHTS = 128
ANY = pl.BlockSpec(memory_space=pl.ANY)


def rows_of(ref, lead, a):
    return ref[:, a * BLK:(a + 1) * BLK] if lead is None else ref[lead, :, a * BLK:(a + 1) * BLK]


def matmul_t(left_t, x):
    return lax.dot_general(left_t, x, (((1,), (1,)), ((), ())), preferred_element_type=F32)


def transposed(ref):
    return ref[...].astype(F32).T.astype(BF16)


def first_last_kernel(tok_hbm, ker_hbm, left_ref, up_ref, down_ref, *refs):
    out_hbms, (work_ref, tok_ref, ker_ref, out_ref, in_sems, out_sems) = refs[:4], refs[4:]
    own_z, own_x, own_core = lax.axis_index("z_hi"), lax.axis_index("x"), lax.axis_index("core")
    loads, stores = [], []
    for quad in range(ROWS // 4):
        lanes = pl.ds(quad * 4 * BLK, 4 * BLK)
        loads.append(pltpu.make_async_copy(ker_hbm.at[:, lanes], ker_ref.at[:, lanes], in_sems.at[2 * quad]))
        loads.append(pltpu.make_async_copy(tok_hbm.at[2, :, lanes], tok_ref.at[:, lanes], in_sems.at[2 * quad + 1]))
    for load in loads:
        load.start()
    left_t = transposed(left_ref)
    for quad in range(ROWS // 4):
        for load in loads[2 * quad:2 * quad + 2]:
            load.wait()
        rows = range(quad * 4, quad * 4 + 4)
        taps = jnp.concatenate([rows_of(ker_ref, None, a) for a in rows], axis=0).astype(F32).T
        prod = matmul_t(left_t, jnp.concatenate([rows_of(tok_ref, None, a) for a in rows], axis=0)) * taps
        for i, a in enumerate(rows):
            one = prod[:, i * CH:(i + 1) * CH].reshape(SEQ, 2, 8, CH)
            for jh in range(2):
                work_ref[a * 256:(a + 1) * 256, jh * CH:(jh + 1) * CH] = one[:, jh].reshape(256, CH)
    own_y = lax.axis_index("y")
    for step in range(4):
        for kind, ref in enumerate((up_ref, down_ref)):
            for i in range(2):
                out_ref[step, 8 + kind, :, i * 256:(i + 1) * 256] = ref[own_y, i * 16:(i + 1) * 16, :]
        for x_step in range(4):
            for core_step in range(2):
                core = own_core if core_step == 0 else 1 - own_core
                dst = lax.rem(own_z + step, 4) * 8 + lax.rem(own_x + x_step, 4) * 2 + core
                for jq in range(4):
                    both = [work_ref[pl.ds(dst * 8 + (jm * 4 + jq), 8, stride=256), :] for jm in range(2)]
                    block = jnp.concatenate(both, axis=0).astype(BF16)
                    out_ref[step, x_step * 2 + core_step, :, jq * 128:(jq + 1) * 128] = block
        stores.append(pltpu.make_async_copy(out_ref.at[step], out_hbms[step], out_sems.at[step]))
        stores[step].start()
    for store in stores:
        store.wait()


def first_pair_kernel(tok_ref, ker_ref, left_ref, out_ref, work_ref):
    left_t = transposed(left_ref)
    for quad in range(ROWS // 4):
        rows = range(quad * 4, quad * 4 + 4)
        taps = jnp.concatenate([rows_of(ker_ref, None, a) for a in rows], axis=0).astype(F32).T
        for i in range(2):
            two = [quad * 4 + 2 * i, quad * 4 + 2 * i + 1]
            prod = matmul_t(left_t, jnp.concatenate([rows_of(tok_ref, n, a) for a in two for n in range(2)], axis=0))
            for k, a in enumerate(two):
                tap = taps[:, (2 * i + k) * CH:(2 * i + k + 1) * CH]
                tap2 = jnp.concatenate([tap, tap], axis=1)
                work_ref[a * BLK:(a + 1) * BLK, :] = prod[:, k * 128:(k + 1) * 128] * tap2
    for dst in range(SEQ):
        for jl in range(8):
            both = [work_ref[pl.ds(dst * 16 + jh * 8 + jl, 8, stride=BLK), :] for jh in range(2)]
            out_ref[dst, :, jl * 128:(jl + 1) * 128] = jnp.concatenate(both, axis=0).astype(BF16)


def z_join_kernel(*refs):
    parts, outs, weights = refs[:4], refs[4:8], refs[8]
    for step, part in enumerate(parts):
        for x_step, out in enumerate(outs):
            for core_step in range(2):
                out[core_step * 4 + step] = part[x_step * 2 + core_step]
        weights[2 * step:2 * step + 2] = part[8:10]


def plane_join_kernel(*refs):
    parts, weights, out, joined = refs[:4], refs[4:8], refs[8], refs[9]
    for i, part in enumerate(parts):
        out[4 * i:4 * i + 4] = part[4:8]
    for i, part in enumerate(weights):
        joined[8 * i:8 * i + 8] = part[...]


def join_kernel(*refs):
    *parts, out = refs
    size = parts[0].shape[0]
    for i, part in enumerate(parts):
        out[size * i:size * (i + 1)] = part[...]


def gate(x, mixed):
    x = x.astype(F32)
    return (x + (0.5 * jnp.tanh(0.5 * x) + 0.5) * mixed).astype(BF16)


def mix(rows, wide):
    return lax.dot_general(rows, wide, (((0,), (0,)), ((), ())), preferred_element_type=F32)


def second_last_kernel(*refs):
    parts, far_ref, right_ref, tok_hbm, out_ref, wide_ref, copy_ref, tok_ref, sem = refs[:4], *refs[4:]
    own_z, own_x, own_core = lax.axis_index("z_hi"), lax.axis_index("x"), lax.axis_index("core")
    load = pltpu.make_async_copy(tok_hbm.at[2], tok_ref, sem)
    load.start()
    wide_ref[...] = jnp.zeros_like(wide_ref)
    copy_ref[...] = right_ref[...].astype(F32)
    for i in range(32):
        core = own_core if i < 16 else 1 - own_core
        x, z = lax.rem(own_x + 4 - i // 4 % 4, 4), lax.rem(own_z + 4 - i % 4, 4)
        at = pl.multiple_of((z * 8 + x * 2 + core) * 8, 8)
        rows = copy_ref[pl.ds(at, 8), :]
        wide_ref[i * 16:i * 16 + 8, :BROWS] = rows
        wide_ref[i * 16 + 8:i * 16 + 16, BROWS:] = rows
    wide = wide_ref[...].astype(BF16)
    load.wait()
    for jq in range(4):
        lanes = slice(jq * 128, (jq + 1) * 128)
        rows = [part[:4, :, lanes].reshape(64, 128) for part in parts] + [far_ref[:, :, lanes].reshape(256, 128)]
        mixed = mix(jnp.concatenate(rows, axis=0), wide)
        for jh in range(2):
            for jm in range(2):
                j = jh * 8 + jm * 4 + jq
                x = tok_ref[:, j * BROWS:(j + 1) * BROWS]
                out_ref[jh, jm * 4 + jq] = gate(x, mixed[jh * CH:(jh + 1) * CH, jm * BROWS:(jm + 1) * BROWS])


def second_pair_kernel(mid_hbm, right_ref, tok_ref, kept_hbm, out_hbm, mid_ref, out_ref, in_sems, out_sems):
    loads, stores = [], []
    for i in range(4):
        at = pl.ds(i * 256, 256)
        loads.append(pltpu.make_async_copy(mid_hbm.at[:, :, at], mid_ref.at[i], in_sems.at[i]))
        loads[i].start()
    right = right_ref[...].astype(F32).reshape(SEQ, ROWS, BROWS)
    zero = jnp.zeros_like(right)
    upper = jnp.concatenate([right, zero], axis=1).reshape(512, BROWS)
    lower = jnp.concatenate([zero, right], axis=1).reshape(512, BROWS)
    wide = jnp.concatenate([upper, lower], axis=1).astype(BF16)
    for jl in range(8):
        if jl % 2 == 0:
            loads[jl // 2].wait()
        lane = jl % 2 * 128
        mixed = mix(mid_ref[jl // 2, :, :, lane:lane + 128].reshape(512, 128), wide)
        for n in range(2):
            for jh in range(2):
                j = jh * 8 + jl
                x = tok_ref[n, :, j * BROWS:(j + 1) * BROWS]
                value = mixed[n * CH:(n + 1) * CH, jh * BROWS:(jh + 1) * BROWS]
                out_ref[jl, jh, :, n * BROWS:(n + 1) * BROWS] = gate(x, value)
        out_at = out_hbm.at[:, jl, :, pl.ds(0, 2 * BROWS)]
        stores.append(pltpu.make_async_copy(out_ref.at[jl], out_at, out_sems.at[jl]))
        stores[jl].start()
    for store in stores:
        store.wait()


def twice_gelu(x):
    return x + x * jnp.tanh(x * (0.7978845608028654 + 0.035677408136300125 * (x * x)))


def mlp_kernel(x_hbm, gain_ref, near_hbm, far_hbm, out_hbm, x_ref, rows_ref, normed_ref, out_ref, weight_ref, *sems):
    in_sems, weight_sems, out_sems = sems
    loads = [
        pltpu.make_async_copy(x_hbm.at[:, :, pl.ds(n * BROWS, BROWS)], x_ref.at[n], in_sems.at[n]) for n in range(3)
    ]
    weights = [
        pltpu.make_async_copy(share, weight_ref.at[pl.ds(core * WEIGHTS, WEIGHTS)], weight_sems.at[core])
        for core, share in enumerate((near_hbm, far_hbm))
    ]
    for load in loads + weights:
        load.start()
    for n, load in enumerate(loads):
        load.wait()
        rows = x_ref[n].reshape(CHAN * CH, BROWS).T
        x = rows.astype(F32)
        mean = jnp.mean(x, axis=1, keepdims=True)
        cent = x - mean
        var = jnp.mean(cent * cent, axis=1, keepdims=True)
        normed = (cent * lax.rsqrt(var + 1e-05) * gain_ref[...]).astype(BF16)
        rows_ref[n * BROWS:(n + 1) * BROWS, :] = rows
        normed_ref[n * BROWS:(n + 1) * BROWS, :] = normed
    own_y, own_z = lax.axis_index("y"), lax.axis_index("z_hi")

    def weight(y, z, kind):
        base = lax.rem(own_y + 4 - y, 4) * 8 + lax.rem(own_z + 4 - z, 4) * 2 + kind
        blocks = [weight_ref[base + step * 32] for step in range(8)]
        return jnp.concatenate([block[:, i * 256:(i + 1) * 256] for block in blocks for i in range(2)], axis=0)

    for load in weights:
        load.wait()
    stores = []
    for h in range(GROUPS):
        lanes = slice(h * 256, (h + 1) * 256)
        hidden = [
            twice_gelu(matmul_t(normed_ref[:, g * 256:(g + 1) * 256], weight(g, h, 0))).astype(BF16)
            for g in range(GROUPS)
        ]
        down = jnp.concatenate([weight(h, g, 1) for g in range(GROUPS)], axis=0)
        acc = jnp.dot(jnp.concatenate(hidden, axis=1), down, preferred_element_type=F32)
        out = (rows_ref[:, lanes].astype(F32) + 0.5 * acc).astype(BF16)
        out_ref[:, :, lanes] = out.reshape(3, BROWS, 256)
        at = pl.ds(h * 256, 256)
        stores.append(pltpu.make_async_copy(out_ref.at[:, :, at], out_hbm.at[:, :, at], out_sems.at[h]))
        stores[h].start()
    for store in stores:
        store.wait()


def shift(x, axis, step, size=4):
    return lax.ppermute(x, axis, [(i, (i + step) % size) for i in range(size)])


def spread(parts, axis):
    return [parts[0]] + [shift(parts[step], axis, step) for step in (1, 2, 3)]


def shape(*dims):
    return jax.ShapeDtypeStruct(dims, BF16)


def whole(*dims):
    return pl.BlockSpec(dims, lambda i: (0,) * len(dims))


def join(kernel, out_shape, name, *args, flops=0):
    return pl.pallas_call(
        kernel,
        out_shape=out_shape,
        compiler_params=pltpu.CompilerParams(vmem_limit_bytes=16 * 1024 * 1024),
        cost_estimate=pl.CostEstimate(flops=flops, bytes_accessed=0, transcendentals=0),
        name=name,
    )(*args)


def per_device(tokens, kernel, left_factor, right_factor, norm_gain, up_weight, down_weight):
    chans = tokens.shape[1]
    local = tokens.shape[2]
    parts = pl.pallas_call(
        first_last_kernel,
        grid=(1,),
        in_specs=[
            ANY,
            ANY,
            whole(BLK, BLK),
            whole(GROUPS, 32, 256),
            whole(GROUPS, 32, 256),
        ],
        out_specs=[ANY] * 4,
        out_shape=[shape(10, 16, 512)] * 4,
        scratch_shapes=[
            pltpu.VMEM((ROWS * 256, 128), F32),
            pltpu.VMEM((chans, local), BF16),
            pltpu.VMEM((chans, local), BF16),
            pltpu.VMEM((4, 10, 16, 512), BF16),
            pltpu.SemaphoreType.DMA((4,)),
            pltpu.SemaphoreType.DMA((4,)),
        ],
        compiler_params=PARAMS,
        name="first_last",
    )(tokens, kernel, left_factor, up_weight.transpose(0, 2, 1), down_weight)
    parts = spread(parts, "z_hi")
    middle = pl.pallas_call(
        first_pair_kernel,
        grid=(1,),
        in_specs=[
            pl.BlockSpec((2, chans, local), lambda i: (0, 0, 0)),
            whole(chans, local),
            whole(BLK, BLK),
        ],
        out_specs=whole(SEQ, 16, 1024),
        out_shape=shape(SEQ, 16, 1024),
        scratch_shapes=[pltpu.VMEM((ROWS * BLK, 128), F32)],
        compiler_params=PARAMS,
        name="first_pair",
    )(tokens, kernel, left_factor)
    middle = lax.all_to_all(middle, SEQ_AXES, 0, 0, tiled=True)

    *parts, weights = join(z_join_kernel, [shape(8, 16, 512)] * 5, "z_join", *parts, flops=200 * 10**9)
    parts = spread(parts, "x")
    weights = spread([weights] * 4, "y")
    blocks, weights = join(plane_join_kernel, [shape(16, 16, 512), shape(32, 16, 512)], "plane_join", *parts, *weights)
    blocks = lax.ppermute(blocks, "core", [(0, 1), (1, 0)])
    blocks, weights = lax.optimization_barrier((blocks, weights))
    near = join(join_kernel, shape(WEIGHTS, 16, 512), "x_join", *spread([weights] * 4, "x"), flops=200 * 10**9)
    far = lax.ppermute(near, "core", [(0, 1), (1, 0)])

    gated = pl.pallas_call(
        second_last_kernel,
        grid=(1,),
        in_specs=[
            whole(8, 16, 512),
            whole(8, 16, 512),
            whole(8, 16, 512),
            whole(8, 16, 512),
            whole(16, 16, 512),
            whole(BROWS, BROWS),
            ANY,
        ],
        out_specs=pl.BlockSpec((2, 8, CH, BROWS), lambda i: (0, 0, 0, 2)),
        out_shape=shape(2, 8, CH, 3 * BROWS),
        scratch_shapes=[
            pltpu.VMEM((512, 512), F32),
            pltpu.VMEM((BROWS, BROWS), F32),
            pltpu.VMEM((chans, local), BF16),
            pltpu.SemaphoreType.DMA,
        ],
        compiler_params=SMALL,
        name="second_last",
    )(*parts, blocks, right_factor, tokens)
    gated = pl.pallas_call(
        second_pair_kernel,
        grid=(1,),
        in_specs=[
            ANY,
            whole(BROWS, BROWS),
            pl.BlockSpec((2, chans, local), lambda i: (0, 0, 0)),
            ANY,
        ],
        out_specs=ANY,
        out_shape=shape(2, 8, CH, 3 * BROWS),
        input_output_aliases={3: 0},
        scratch_shapes=[
            pltpu.VMEM((4, SEQ, 16, 256), BF16),
            pltpu.VMEM((8, 2, CH, 2 * BROWS), BF16),
            pltpu.SemaphoreType.DMA((4,)),
            pltpu.SemaphoreType.DMA((8,)),
        ],
        compiler_params=SMALL,
        name="second_pair",
    )(middle, right_factor, tokens, gated)
    gated = gated.reshape(CHAN, CH, 3 * BROWS)
    gated = lax.all_to_all(gated, CHAN_AXES, 0, 0, tiled=True)
    vmem = pl.BlockSpec(memory_space=pltpu.VMEM)
    width = CHAN * CH
    return pl.pallas_call(
        mlp_kernel,
        in_specs=[ANY, vmem, ANY, ANY],
        out_specs=ANY,
        out_shape=shape(3, BROWS, width),
        scratch_shapes=[
            pltpu.VMEM((3, CHAN, CH, BROWS), BF16),
            pltpu.VMEM((3 * BROWS, width), BF16),
            pltpu.VMEM((3 * BROWS, width), BF16),
            pltpu.VMEM((3, BROWS, width), BF16),
            pltpu.VMEM((2 * WEIGHTS, 16, 512), BF16),
            pltpu.SemaphoreType.DMA((3,)),
            pltpu.SemaphoreType.DMA((2,)),
            pltpu.SemaphoreType.DMA((GROUPS,)),
        ],
        compiler_params=PARAMS,
        name="mlp",
    )(gated, norm_gain.reshape(1, width), near, far)


def solution(mesh):
    fine = jax.sharding.Mesh(mesh.devices.reshape(4, 4, 2, 4, 4), SEQ_AXES + CHAN_AXES)
    placed = (
        P(None, CHAN_AXES, SEQ_AXES),
        P(CHAN_AXES, SEQ_AXES),
        P(),
        P(),
        P(),
        P(None, None, SEQ_AXES),
        P(None, SEQ_AXES, None),
    )
    return jax.shard_map(
        per_device,
        mesh=fine,
        in_specs=placed,
        out_specs=P(None, SEQ_AXES + CHAN_AXES, None),
        check_vma=False,
    )
```

```python
import jax
import jax.numpy as jnp
from jax import lax
from jax.experimental import pallas as pl
from jax.experimental.pallas import tpu as pltpu
from jax.sharding import PartitionSpec as P

F32 = jnp.float32
BF16 = jnp.bfloat16
SEQ = 32
CHAN = 16
ROWS = 8
BLK = 512
BROWS = 256
CH = 64
GROUPS = 4
SEQ_AXES = ("z_hi", "x", "core")
CHAN_AXES = ("z_lo", "y")
PARAMS = pltpu.CompilerParams(vmem_limit_bytes=60 * 1024 * 1024)
SMALL = pltpu.CompilerParams(vmem_limit_bytes=24 * 1024 * 1024)
WEIGHTS = 128
ANY = pl.BlockSpec(memory_space=pl.ANY)


def rows_of(ref, lead, a):
    return ref[:, a * BLK:(a + 1) * BLK] if lead is None else ref[lead, :, a * BLK:(a + 1) * BLK]


def matmul_t(left_t, x):
    return lax.dot_general(left_t, x, (((1,), (1,)), ((), ())), preferred_element_type=F32)


def transposed(ref):
    return ref[...].astype(F32).T.astype(BF16)


def first_last_kernel(tok_ref, ker_ref, left_ref, up_ref, down_ref, *refs):
    *outs, work_ref = refs
    own_z, own_x, own_core = lax.axis_index("z_hi"), lax.axis_index("x"), lax.axis_index("core")
    left_t = transposed(left_ref)
    for quad in range(ROWS // 4):
        rows = range(quad * 4, quad * 4 + 4)
        taps = jnp.concatenate([rows_of(ker_ref, None, a) for a in rows], axis=0).astype(F32).T
        prod = matmul_t(left_t, jnp.concatenate([rows_of(tok_ref, 0, a) for a in rows], axis=0)) * taps
        for i, a in enumerate(rows):
            one = prod[:, i * CH:(i + 1) * CH].reshape(SEQ, 2, 8, CH)
            for jh in range(2):
                work_ref[a * 256:(a + 1) * 256, jh * CH:(jh + 1) * CH] = one[:, jh].reshape(256, CH)
    own_y = lax.axis_index("y")
    for step in range(4):
        for kind, ref in enumerate((up_ref, down_ref)):
            for i in range(2):
                outs[step][8 + kind, :, i * 256:(i + 1) * 256] = ref[own_y, i * 16:(i + 1) * 16, :]
        for x_step in range(4):
            for core_step in range(2):
                core = own_core if core_step == 0 else 1 - own_core
                dst = lax.rem(own_z + step, 4) * 8 + lax.rem(own_x + x_step, 4) * 2 + core
                for jq in range(4):
                    both = [work_ref[pl.ds(dst * 8 + (jm * 4 + jq), 8, stride=256), :] for jm in range(2)]
                    block = jnp.concatenate(both, axis=0).astype(BF16)
                    outs[step][x_step * 2 + core_step, :, jq * 128:(jq + 1) * 128] = block


def first_pair_kernel(tok_ref, ker_ref, left_ref, out_ref, work_ref):
    left_t = transposed(left_ref)
    for quad in range(ROWS // 4):
        rows = range(quad * 4, quad * 4 + 4)
        taps = jnp.concatenate([rows_of(ker_ref, None, a) for a in rows], axis=0).astype(F32).T
        for i in range(2):
            two = [quad * 4 + 2 * i, quad * 4 + 2 * i + 1]
            prod = matmul_t(left_t, jnp.concatenate([rows_of(tok_ref, n, a) for a in two for n in range(2)], axis=0))
            for k, a in enumerate(two):
                tap = taps[:, (2 * i + k) * CH:(2 * i + k + 1) * CH]
                tap2 = jnp.concatenate([tap, tap], axis=1)
                work_ref[a * BLK:(a + 1) * BLK, :] = prod[:, k * 128:(k + 1) * 128] * tap2
    for dst in range(SEQ):
        for jl in range(8):
            both = [work_ref[pl.ds(dst * 16 + jh * 8 + jl, 8, stride=BLK), :] for jh in range(2)]
            out_ref[dst, :, jl * 128:(jl + 1) * 128] = jnp.concatenate(both, axis=0).astype(BF16)


def z_join_kernel(*refs):
    parts, outs, weights = refs[:4], refs[4:8], refs[8]
    for step, part in enumerate(parts):
        for x_step, out in enumerate(outs):
            for core_step in range(2):
                out[core_step * 4 + step] = part[x_step * 2 + core_step]
        weights[2 * step:2 * step + 2] = part[8:10]


def plane_join_kernel(*refs):
    parts, weights, out, joined = refs[:4], refs[4:8], refs[8], refs[9]
    for i, part in enumerate(parts):
        out[4 * i:4 * i + 4] = part[4:8]
    for i, part in enumerate(weights):
        joined[8 * i:8 * i + 8] = part[...]


def join_kernel(*refs):
    *parts, out = refs
    size = parts[0].shape[0]
    for i, part in enumerate(parts):
        out[size * i:size * (i + 1)] = part[...]


def gate(x, mixed):
    x = x.astype(F32)
    return (x + (0.5 * jnp.tanh(0.5 * x) + 0.5) * mixed).astype(BF16)


def mix(rows, wide):
    return lax.dot_general(rows, wide, (((0,), (0,)), ((), ())), preferred_element_type=F32)


def second_last_kernel(*refs):
    parts, far_ref, right_ref, tok_hbm, out_ref, wide_ref, copy_ref, tok_ref, sem = refs[:4], *refs[4:]
    own_z, own_x, own_core = lax.axis_index("z_hi"), lax.axis_index("x"), lax.axis_index("core")
    load = pltpu.make_async_copy(tok_hbm.at[2], tok_ref, sem)
    load.start()
    wide_ref[...] = jnp.zeros_like(wide_ref)
    copy_ref[...] = right_ref[...].astype(F32)
    for i in range(32):
        core = own_core if i < 16 else 1 - own_core
        x, z = lax.rem(own_x + 4 - i // 4 % 4, 4), lax.rem(own_z + 4 - i % 4, 4)
        at = pl.multiple_of((z * 8 + x * 2 + core) * 8, 8)
        rows = copy_ref[pl.ds(at, 8), :]
        wide_ref[i * 16:i * 16 + 8, :BROWS] = rows
        wide_ref[i * 16 + 8:i * 16 + 16, BROWS:] = rows
    wide = wide_ref[...].astype(BF16)
    load.wait()
    for jq in range(4):
        lanes = slice(jq * 128, (jq + 1) * 128)
        rows = [part[:4, :, lanes].reshape(64, 128) for part in parts] + [far_ref[:, :, lanes].reshape(256, 128)]
        mixed = mix(jnp.concatenate(rows, axis=0), wide)
        for jh in range(2):
            for jm in range(2):
                j = jh * 8 + jm * 4 + jq
                x = tok_ref[:, j * BROWS:(j + 1) * BROWS]
                out_ref[jh, jm * 4 + jq] = gate(x, mixed[jh * CH:(jh + 1) * CH, jm * BROWS:(jm + 1) * BROWS])


def second_pair_kernel(mid_ref, right_ref, tok_ref, kept_ref, out_ref):
    right = right_ref[...].astype(F32).reshape(SEQ, ROWS, BROWS)
    zero = jnp.zeros_like(right)
    upper = jnp.concatenate([right, zero], axis=1).reshape(512, BROWS)
    lower = jnp.concatenate([zero, right], axis=1).reshape(512, BROWS)
    wide = jnp.concatenate([upper, lower], axis=1).astype(BF16)
    for jl in range(8):
        mixed = mix(mid_ref[:, :, jl * 128:(jl + 1) * 128].reshape(512, 128), wide)
        for n in range(2):
            for jh in range(2):
                j = jh * 8 + jl
                x = tok_ref[n, :, j * BROWS:(j + 1) * BROWS]
                value = mixed[n * CH:(n + 1) * CH, jh * BROWS:(jh + 1) * BROWS]
                out_ref[jh, jl, :, n * BROWS:(n + 1) * BROWS] = gate(x, value)


def twice_gelu(x):
    return x + x * jnp.tanh(x * (0.7978845608028654 + 0.035677408136300125 * (x * x)))


def mlp_kernel(x_hbm, gain_ref, near_hbm, far_hbm, out_hbm, x_ref, rows_ref, normed_ref, out_ref, weight_ref, acc_ref, *sems):
    in_sems, weight_sems, out_sems = sems
    loads = [
        pltpu.make_async_copy(x_hbm.at[:, :, pl.ds(n * BROWS, BROWS)], x_ref.at[n], in_sems.at[n]) for n in range(3)
    ]
    weights = [
        pltpu.make_async_copy(share, weight_ref.at[pl.ds(core * WEIGHTS, WEIGHTS)], weight_sems.at[core])
        for core, share in enumerate((near_hbm, far_hbm))
    ]
    for load in loads + weights:
        load.start()
    for n, load in enumerate(loads):
        load.wait()
        rows = x_ref[n].reshape(CHAN * CH, BROWS).T
        x = rows.astype(F32)
        mean = jnp.mean(x, axis=1, keepdims=True)
        cent = x - mean
        var = jnp.mean(cent * cent, axis=1, keepdims=True)
        normed = (cent * lax.rsqrt(var + 1e-05) * gain_ref[...]).astype(BF16)
        rows_ref[n * BROWS:(n + 1) * BROWS, :] = rows
        normed_ref[n * BROWS:(n + 1) * BROWS, :] = normed
    own_y, own_z = lax.axis_index("y"), lax.axis_index("z_hi")

    def half(y, z, kind, core):
        base = lax.rem(own_y + 4 - y, 4) * 8 + lax.rem(own_z + 4 - z, 4) * 2 + kind + core * WEIGHTS
        blocks = [weight_ref[base + x_step * 32] for x_step in range(4)]
        return jnp.concatenate([block[:, i * 256:(i + 1) * 256] for block in blocks for i in range(2)], axis=0)

    stores = []
    for core in range(2):
        weights[core].wait()
        for pair in range(2):
            hidden = []
            for g in range(GROUPS):
                up = jnp.concatenate([half(g, pair * 2 + k, 0, core) for k in range(2)], axis=0)
                hidden.append(twice_gelu(matmul_t(normed_ref[:, g * 256:(g + 1) * 256], up)).astype(BF16))
            for k in range(2):
                h = pair * 2 + k
                lanes = slice(h * 256, (h + 1) * 256)
                down = jnp.concatenate([half(h, g, 1, core) for g in range(GROUPS)], axis=0)
                mine = jnp.concatenate([part[:, k * 128:(k + 1) * 128] for part in hidden], axis=1)
                term = jnp.dot(mine, down, preferred_element_type=F32)
                if core == 0:
                    acc_ref[h] = term
                    continue
                out = (rows_ref[:, lanes].astype(F32) + 0.5 * (acc_ref[h] + term)).astype(BF16)
                out_ref[:, :, lanes] = out.reshape(3, BROWS, 256)
                at = pl.ds(h * 256, 256)
                stores.append(pltpu.make_async_copy(out_ref.at[:, :, at], out_hbm.at[:, :, at], out_sems.at[h]))
                stores[h].start()
    for store in stores:
        store.wait()


def shift(x, axis, step, size=4):
    return lax.ppermute(x, axis, [(i, (i + step) % size) for i in range(size)])


def spread(parts, axis):
    return [parts[0]] + [shift(parts[step], axis, step) for step in (1, 2, 3)]


def shape(*dims):
    return jax.ShapeDtypeStruct(dims, BF16)


def whole(*dims):
    return pl.BlockSpec(dims, lambda i: (0,) * len(dims))


def join(kernel, out_shape, name, *args, flops=0):
    return pl.pallas_call(
        kernel,
        out_shape=out_shape,
        compiler_params=pltpu.CompilerParams(vmem_limit_bytes=16 * 1024 * 1024),
        cost_estimate=pl.CostEstimate(flops=flops, bytes_accessed=0, transcendentals=0),
        name=name,
    )(*args)


def per_device(tokens, kernel, left_factor, right_factor, norm_gain, up_weight, down_weight):
    chans = tokens.shape[1]
    local = tokens.shape[2]
    parts = pl.pallas_call(
        first_last_kernel,
        grid=(1,),
        in_specs=[
            pl.BlockSpec((1, chans, local), lambda i: (2, 0, 0)),
            whole(chans, local),
            whole(BLK, BLK),
            whole(GROUPS, 32, 256),
            whole(GROUPS, 32, 256),
        ],
        out_specs=[whole(10, 16, 512)] * 4,
        out_shape=[shape(10, 16, 512)] * 4,
        scratch_shapes=[pltpu.VMEM((ROWS * 256, 128), F32)],
        compiler_params=PARAMS,
        name="first_last",
    )(tokens, kernel, left_factor, up_weight.transpose(0, 2, 1), down_weight)
    parts = spread(parts, "z_hi")
    middle = pl.pallas_call(
        first_pair_kernel,
        grid=(1,),
        in_specs=[
            pl.BlockSpec((2, chans, local), lambda i: (0, 0, 0)),
            whole(chans, local),
            whole(BLK, BLK),
        ],
        out_specs=whole(SEQ, 16, 1024),
        out_shape=shape(SEQ, 16, 1024),
        scratch_shapes=[pltpu.VMEM((ROWS * BLK, 128), F32)],
        compiler_params=PARAMS,
        name="first_pair",
    )(tokens, kernel, left_factor)
    middle = lax.all_to_all(middle, SEQ_AXES, 0, 0, tiled=True)

    *parts, weights = join(z_join_kernel, [shape(8, 16, 512)] * 5, "z_join", *parts, flops=200 * 10**9)
    parts = spread(parts, "x")
    weights = spread([weights] * 4, "y")
    blocks, weights = join(plane_join_kernel, [shape(16, 16, 512), shape(32, 16, 512)], "plane_join", *parts, *weights)
    blocks = lax.ppermute(blocks, "core", [(0, 1), (1, 0)])
    blocks, weights = lax.optimization_barrier((blocks, weights))
    near = join(join_kernel, shape(WEIGHTS, 16, 512), "x_join", *spread([weights] * 4, "x"), flops=200 * 10**9)
    far = lax.ppermute(near, "core", [(0, 1), (1, 0)])

    gated = pl.pallas_call(
        second_last_kernel,
        grid=(1,),
        in_specs=[
            whole(8, 16, 512),
            whole(8, 16, 512),
            whole(8, 16, 512),
            whole(8, 16, 512),
            whole(16, 16, 512),
            whole(BROWS, BROWS),
            ANY,
        ],
        out_specs=pl.BlockSpec((2, 8, CH, BROWS), lambda i: (0, 0, 0, 2)),
        out_shape=shape(2, 8, CH, 3 * BROWS),
        scratch_shapes=[
            pltpu.VMEM((512, 512), F32),
            pltpu.VMEM((BROWS, BROWS), F32),
            pltpu.VMEM((chans, local), BF16),
            pltpu.SemaphoreType.DMA,
        ],
        compiler_params=SMALL,
        name="second_last",
    )(*parts, blocks, right_factor, tokens)
    gated = pl.pallas_call(
        second_pair_kernel,
        grid=(1,),
        in_specs=[
            whole(SEQ, 16, 1024),
            whole(BROWS, BROWS),
            pl.BlockSpec((2, chans, local), lambda i: (0, 0, 0)),
            ANY,
        ],
        out_specs=pl.BlockSpec((2, 8, CH, 2 * BROWS), lambda i: (0, 0, 0, 0)),
        out_shape=shape(2, 8, CH, 3 * BROWS),
        input_output_aliases={3: 0},
        compiler_params=SMALL,
        name="second_pair",
    )(middle, right_factor, tokens, gated)
    gated = gated.reshape(CHAN, CH, 3 * BROWS)
    gated = lax.all_to_all(gated, CHAN_AXES, 0, 0, tiled=True)
    vmem = pl.BlockSpec(memory_space=pltpu.VMEM)
    width = CHAN * CH
    return pl.pallas_call(
        mlp_kernel,
        in_specs=[ANY, vmem, ANY, ANY],
        out_specs=ANY,
        out_shape=shape(3, BROWS, width),
        scratch_shapes=[
            pltpu.VMEM((3, CHAN, CH, BROWS), BF16),
            pltpu.VMEM((3 * BROWS, width), BF16),
            pltpu.VMEM((3 * BROWS, width), BF16),
            pltpu.VMEM((3, BROWS, width), BF16),
            pltpu.VMEM((2 * WEIGHTS, 16, 512), BF16),
            pltpu.VMEM((GROUPS, 3 * BROWS, 256), F32),
            pltpu.SemaphoreType.DMA((3,)),
            pltpu.SemaphoreType.DMA((2,)),
            pltpu.SemaphoreType.DMA((GROUPS,)),
        ],
        compiler_params=PARAMS,
        name="mlp",
    )(gated, norm_gain.reshape(1, width), near, far)


def solution(mesh):
    fine = jax.sharding.Mesh(mesh.devices.reshape(4, 4, 2, 4, 4), SEQ_AXES + CHAN_AXES)
    placed = (
        P(None, CHAN_AXES, SEQ_AXES),
        P(CHAN_AXES, SEQ_AXES),
        P(),
        P(),
        P(),
        P(None, None, SEQ_AXES),
        P(None, SEQ_AXES, None),
    )
    return jax.shard_map(
        per_device,
        mesh=fine,
        in_specs=placed,
        out_specs=P(None, SEQ_AXES + CHAN_AXES, None),
        check_vma=False,
    )
```
